32 devices in a mesh: dp: 8 (over z, x), seq: 4 (over y, core).
Axes of the slice: x: 2, y: 2, z: 4, core: 2. Of those that a mesh axis runs over, the one named last changes fastest.
Arguments:
- layer_input: bfloat16 [16, 2048, 768], P('dp', 'seq'), may hold values from -6 to 6
- cotangent: bfloat16 [16, 2048, 768], P('dp', 'seq'), may hold values from -6 to 6
- norm_gain1: bfloat16 [768], P('dp'), may hold values from 0.099609375 to 1.8984375
- w_qkv: bfloat16 [768, 2304], P('dp'), may hold values from -0.21875 to 0.21875
- w_out: bfloat16 [768, 768], P('dp'), may hold values from -6 to 6
- norm_gain2: bfloat16 [768], P('dp'), may hold values from 0.099609375 to 1.8984375
- w_in: bfloat16 [768, 2304], P('dp'), may hold values from -0.21875 to 0.21875
- w_down: bfloat16 [1152, 768], P(None, 'dp'), may hold values from -0.1875 to 0.1875
Outputs:
- output: bfloat16 [16, 2048, 768], P('dp', 'seq')
- grad_input: float32 [16, 2048, 768], P('dp', 'seq')
- grad_gain1: float32 [768], P('dp')
- grad_qkv: float32 [768, 2304], P('dp')
- grad_out: float32 [768, 768], P('dp')
- grad_gain2: float32 [768], P('dp')
- grad_in: float32 [768, 2304], P('dp')
- grad_down: float32 [1152, 768], P(None, 'dp')
The draws below stay inside these ranges and needn't reach their ends.
All inputs are finite; a program needn't handle non-finite values.
Results may differ from the reference program's by a relative error of at most 0.017.
Values may be sent and summed in bfloat16 or wider, within the bound.
A program may use at most 128 MiB of HBM per device.

```python
import math
import jax
import jax.numpy as jnp
from jax import lax

D = 768
H = 12
HD = 64
FF = 1152
SEQ_LEN = 2048
SEQS = 2
SEQUENCES = 16
N_DP = 8


def with_spikes(values, stream_key, source, target, shards_of, factor):
    def block_of(dim):
        return (jnp.arange(values.shape[dim]) // (values.shape[dim] // shards_of)).reshape((-1,) + (1,) * (values.ndim - 1 - dim))

    first = jax.random.permutation(stream_key, shards_of)[block_of(target)]
    other_side = (block_of(target) + shards_of // 2) % shards_of
    return jnp.where((block_of(source) == first) | (block_of(source) == other_side), factor * values, values)


def block_scale(rng, extent, cuts, least, top_value):
    level, own = 1.0, jax.random.fold_in(rng, 6)
    for axis_at, shards_of in cuts:
        steps = jnp.exp(jax.random.uniform(jax.random.fold_in(own, axis_at), (shards_of,), jnp.float32, least / len(cuts), top_value / len(cuts)))
        level = level * jnp.repeat(steps, extent[axis_at] // shards_of).reshape([-1 if axis == axis_at else 1 for axis in range(len(extent))])
    return level


def centred(rng, shape, width, bound, split=(), kind=jnp.bfloat16):
    drawn = jax.random.normal(rng, shape, jnp.float32) * width
    if len(split) > 0:
        drawn = block_scale(rng, shape, split, -0.22, 0.18) * drawn
    return jnp.clip(drawn, min=-bound, max=bound).astype(kind)


def bell_draw_with(own_key, dims, spread, limit, shards, heavy, held_as=jnp.bfloat16):
    drawn = spread * jax.random.normal(own_key, dims, jnp.float32)
    if shards:
        drawn = drawn * block_scale(own_key, dims, shards, -0.22, 0.18)
    return jnp.clip(with_spikes(drawn, jax.random.fold_in(own_key, 3), *heavy), -limit, limit).astype(held_as)


def setup_inputs(seed: int = 0) -> dict:
    streams_of = jax.random.split(jax.random.key(seed), 9)
    return {
        "layer_input": bell_draw_with(streams_of[0], (SEQUENCES, SEQ_LEN, D), 1.0, 6.0, ((0, 8), (1, 4)), (0, 2, 8, 2.0)),
        "cotangent": bell_draw_with(streams_of[1], (SEQUENCES, SEQ_LEN, D), 1.0, 6.0, ((0, 8), (1, 4)), (0, 2, 8, 2.0)),
        "norm_gain1": jnp.clip(1.0 + 0.18 * jax.random.normal(streams_of[2], (D,), jnp.float32), 0.099609375, 1.8984375).astype(jnp.bfloat16),
        "w_qkv": centred(streams_of[3], (D, 3 * D), D ** -0.5, 0.21875, ((0, 8),)),
        "w_out": centred(streams_of[4], (D, D), (max(1, 3 * D // SEQ_LEN)) ** -0.5, 6.0, ((0, 8),)),
        "norm_gain2": jnp.clip(1.0 + 0.18 * jax.random.normal(streams_of[5], (D,), jnp.float32), 0.099609375, 1.8984375).astype(jnp.bfloat16),
        "w_in": centred(streams_of[6], (D, 2 * FF), D ** -0.5, 0.21875, ((0, 8),)),
        "w_down": centred(streams_of[7], (FF, D), FF ** -0.5, 0.1875, ((1, 8),)),
    }


@jax.custom_vjp
def low(v):
    return lax.optimization_barrier(v.astype(jnp.bfloat16)).astype(jnp.float32)

@jax.custom_vjp
def low_back(v):
    return v

def low_keep(v):
    return (low(v), None)

def low_pass(kept, grad):
    return (grad,)

def back_keep(v):
    return (v, None)

def back_low(kept, grad):
    return (low(grad),)
low.defvjp(low_keep, low_pass)
low_back.defvjp(back_keep, back_low)
rope_base = 160000.0
norm_eps = 1e-05
precise = lax.Precision.HIGHEST

def normalize(values):
    centre = values - lax.optimization_barrier(jnp.mean(values, axis=-1, keepdims=True))
    inverse = lax.rsqrt(lax.optimization_barrier(jnp.mean(centre * centre, axis=-1, keepdims=True)) + norm_eps)
    return centre * inverse

def rope_tables(positions):
    half = HD // 2
    freqs = rope_base ** (-(jnp.arange(half, dtype=jnp.float32) * 2.0) / HD)
    angles = positions.astype(jnp.float32)[:, None] * freqs[None, :]
    angles = jnp.concatenate([angles, angles], axis=-1)
    return (jnp.cos(angles), jnp.sin(angles))

def rotate(values, cosine, sine):
    half = values.shape[-1] // 2
    turned = jnp.concatenate([-values[..., half:], values[..., :half]], axis=-1)
    return values * cosine[:, None, :] + turned * sine[:, None, :]

def layer(inputs, gain_one, proj_qkv, proj_out, gain_two, proj_in, proj_down):
    group = inputs.shape[0]
    attn_in = low(normalize(inputs) * gain_one)
    mixed = low_back(jnp.einsum('gld,de->gle', attn_in, proj_qkv, precision=precise))
    mixed = mixed.reshape(group, SEQ_LEN, 3, H, HD)
    cosine, sine = rope_tables(jnp.arange(SEQ_LEN, dtype=jnp.int32))
    query = low_back(low(rotate(mixed[:, :, 0], cosine, sine)))
    keys = low_back(low(rotate(mixed[:, :, 1], cosine, sine)))
    values = low_back(low(mixed[:, :, 2]))
    block = min(512, SEQ_LEN)
    scale = HD ** (-0.5)

    def one_block(rows):
        scores = low_back(jnp.einsum('gqhd,gkhd->ghqk', rows, keys, precision=precise) * scale)
        probs = jax.nn.softmax(scores, axis=-1)
        return jnp.einsum('ghqk,gkhd->gqhd', low(probs), values, precision=precise)
    blocks = jnp.moveaxis(query.reshape(group, SEQ_LEN // block, block, H, HD), 1, 0)
    attended = jnp.moveaxis(lax.map(jax.checkpoint(one_block), blocks), 0, 1).reshape(group, SEQ_LEN, D)
    attended = low_back(low(attended))
    hidden = inputs + low_back(jnp.einsum('gld,de->gle', attended, proj_out, precision=precise))
    ffn_in = low(normalize(hidden) * gain_two)
    gate_up = low_back(jnp.einsum('gld,de->gle', ffn_in, proj_in, precision=precise))
    product = low(jax.nn.gelu(gate_up[..., :FF], approximate=False) * gate_up[..., FF:])
    return hidden + jnp.einsum('glf,fd->gld', product, proj_down, precision=precise)

def reference(layer_input, cotangent, norm_gain1, w_qkv, w_out, norm_gain2, w_in, w_down):
    weights = tuple((item.astype(jnp.float32) for item in (norm_gain1, w_qkv, w_out, norm_gain2, w_in, w_down)))
    total = SEQS * N_DP
    group = math.gcd(total, max(1, 4096 // SEQ_LEN))
    inputs = layer_input.astype(jnp.float32).reshape(total // group, group, SEQ_LEN, D)
    grads_in = cotangent.astype(jnp.float32).reshape(total // group, group, SEQ_LEN, D)

    def step(carry, pieces):
        seq_in, seq_grad = pieces
        result, pull = jax.vjp(layer, seq_in, *weights)
        pulled = pull(seq_grad)
        carry = tuple((kept_sum + term for kept_sum, term in zip(carry, pulled[1:])))
        return (carry, (result.astype(jnp.bfloat16), pulled[0]))
    zeros = tuple((jnp.zeros_like(item) for item in weights))
    sums, (outputs, grad_inputs) = lax.scan(step, zeros, (inputs, grads_in))
    return (outputs.reshape(total, SEQ_LEN, D), grad_inputs.reshape(total, SEQ_LEN, D), sums[0], sums[1], sums[2], sums[3], sums[4], sums[5])
```

```python
import functools
import math

import jax
import jax.numpy as jnp
from jax import lax
from jax.experimental import pallas as pl
from jax.experimental.pallas import tpu as pltpu
from jax.sharding import PartitionSpec as P

H = 12
HD = 64
FF = 1152


rope_base = 160000.0
norm_eps = 1e-05


def normalize(values):
    centre = values - jnp.mean(values, axis=-1, keepdims=True)
    inverse = lax.rsqrt(jnp.mean(centre * centre, axis=-1, keepdims=True) + norm_eps)
    return (centre * inverse, inverse)


def norm_back(grad_normed, normed, inverse, gain):
    scaled = grad_normed * gain
    first = jnp.mean(scaled, axis=-1, keepdims=True)
    second = jnp.mean(scaled * normed, axis=-1, keepdims=True)
    return inverse * (scaled - first - normed * second)


def rope_tables(positions):
    half = HD // 2
    freqs = rope_base ** (-(jnp.arange(half, dtype=jnp.float32) * 2.0) / HD)
    angles = positions.astype(jnp.float32)[:, None] * freqs[None, :]
    angles = jnp.concatenate([angles, angles], axis=-1)
    return (jnp.cos(angles), jnp.sin(angles))


def rotate(values, cosine, sine):
    half = values.shape[-1] // 2
    turned = jnp.concatenate([-values[..., half:], values[..., :half]], axis=-1)
    return values * cosine[:, None, :] + turned * sine[:, None, :]


def rotate_back(grads, cosine, sine):
    half = grads.shape[-1] // 2
    moved = grads * sine[:, None, :]
    turned = jnp.concatenate([moved[..., half:], -moved[..., :half]], axis=-1)
    return grads * cosine[:, None, :] + turned


def exact_gelu(values):
    return jax.nn.gelu(values, approximate=False)


def contract_rows(left, right):
    return lax.dot_general(
        left, right, (((0,), (0,)), ((), ())), preferred_element_type=jnp.float32
    )


def times_transpose(left, right):
    return lax.dot_general(
        left, right, (((1,), (1,)), ((), ())), preferred_element_type=jnp.float32
    )


SCALE = HD ** (-0.5)
TO_BASE2 = SCALE * math.log2(math.e)
VMEM_LIMIT = 56 * 1024 * 1024


def dot_nt(left, right):
    return lax.dot_general(
        left, right, (((1,), (1,)), ((), ())), preferred_element_type=jnp.float32
    )


def dot_nn(left, right):
    return lax.dot_general(
        left, right, (((1,), (0,)), ((), ())), preferred_element_type=jnp.float32
    )


def only_head(values, head):
    lanes = lax.broadcasted_iota(jnp.int32, values.shape, 1)
    mine = (lanes < HD) if head == 0 else (lanes >= HD)
    return jnp.where(mine, values, jnp.zeros_like(values))


def join_heads(first, second):
    lanes = lax.broadcasted_iota(jnp.int32, first.shape, 1)
    return jnp.where(lanes < HD, first, second)


def attend_kernel(q_ref, k_ref, v_ref, out_ref, lse_ref, wide_ref):
    @pl.when(pl.program_id(1) == 0)
    def _():
        wide_ref[:, : 2 * HD] = v_ref[...]
        wide_ref[:, 2 * HD :] = jnp.ones_like(v_ref)

    outs, sums = [], []
    for head in range(2):
        scores = dot_nt(only_head(q_ref[...], head), k_ref[...])
        top = jnp.max(scores, axis=-1, keepdims=True)
        weights = jnp.exp2((scores - top) * TO_BASE2).astype(jnp.bfloat16)
        both = dot_nn(weights, wide_ref[...])
        total = both[:, 2 * HD :]
        outs.append(both[:, : 2 * HD] / total)
        sums.append(top * TO_BASE2 + jnp.log2(total))
    out_ref[...] = join_heads(outs[0], outs[1]).astype(jnp.bfloat16)
    turned = join_heads(sums[0], sums[1]).T
    lse_ref[0, 0:1, :] = turned[0:1]
    lse_ref[0, 1:2, :] = turned[HD : HD + 1]


def attend(query, keys, values, block):
    rows, width = query.shape
    length = keys.shape[0]
    pairs = width // (2 * HD)
    return pl.pallas_call(
        attend_kernel,
        grid=(pairs, rows // block),
        in_specs=[
            pl.BlockSpec((block, 2 * HD), lambda p, i: (i, p)),
            pl.BlockSpec((length, 2 * HD), lambda p, i: (0, p)),
            pl.BlockSpec((length, 2 * HD), lambda p, i: (0, p + pairs)),
        ],
        out_specs=[
            pl.BlockSpec((block, 2 * HD), lambda p, i: (i, p)),
            pl.BlockSpec((1, 8, block), lambda p, i: (p, 0, i)),
        ],
        out_shape=[
            jax.ShapeDtypeStruct((rows, width), jnp.bfloat16),
            jax.ShapeDtypeStruct((pairs, 8, rows), jnp.float32),
        ],
        scratch_shapes=[pltpu.VMEM((length, 4 * HD), jnp.bfloat16)],
        compiler_params=pltpu.CompilerParams(vmem_limit_bytes=VMEM_LIMIT),
        cost_estimate=pl.CostEstimate(
            flops=16 * rows * length * width,
            bytes_accessed=4 * length * width + 4 * rows * width,
            transcendentals=rows * length * width // HD,
        ),
        name="attend",
    )(query, keys, values)


def attend_back_kernel(
    q_ref, do_ref, o_ref, lse_ref, k_ref, v_ref, dq_ref, dk_ref, dv_ref, acc_ref, delta_ref
):
    step = pl.program_id(1)

    @pl.when(step == 0)
    def _():
        both = (do_ref[...].astype(jnp.float32) * o_ref[...].astype(jnp.float32)).T
        delta_ref[0:1, :] = jnp.sum(both[:HD], axis=0, keepdims=True)
        delta_ref[1:2, :] = jnp.sum(both[HD:], axis=0, keepdims=True)
        acc_ref[...] = jnp.zeros_like(acc_ref)

    keys = k_ref[...]
    turned_keys = keys.astype(jnp.float32).T.astype(jnp.bfloat16)
    grad_keys, grad_values = [], []
    for head in range(2):
        scores = dot_nt(keys, only_head(q_ref[...], head))
        probs = jnp.exp2(scores * TO_BASE2 - lse_ref[0, head : head + 1, :])
        grad_probs = dot_nt(v_ref[...], only_head(do_ref[...], head))
        grad_scores = (probs * (grad_probs - delta_ref[head : head + 1, :])).astype(jnp.bfloat16)
        grad_values.append(dot_nn(probs.astype(jnp.bfloat16), do_ref[...]))
        grad_keys.append(dot_nn(grad_scores, q_ref[...]))
        acc_ref[head * HD : (head + 1) * HD, :] += dot_nn(
            turned_keys[head * HD : (head + 1) * HD], grad_scores
        )
    dv_ref[...] = join_heads(grad_values[0], grad_values[1]).astype(jnp.bfloat16)
    dk_ref[...] = (join_heads(grad_keys[0], grad_keys[1]) * SCALE).astype(jnp.bfloat16)

    @pl.when(step == pl.num_programs(1) - 1)
    def _():
        dq_ref[...] = (acc_ref[...].T * SCALE).astype(jnp.bfloat16)


def attend_back(query, grads, outs, lse, keys, block):
    rows, width = query.shape
    length = keys.shape[0]
    pairs = width // (2 * HD)
    own = pl.BlockSpec((rows, 2 * HD), lambda p, i: (0, p))
    return pl.pallas_call(
        attend_back_kernel,
        grid=(pairs, length // block),
        in_specs=[
            own,
            own,
            own,
            pl.BlockSpec((1, 8, rows), lambda p, i: (p, 0, 0)),
            pl.BlockSpec((block, 2 * HD), lambda p, i: (i, p)),
            pl.BlockSpec((block, 2 * HD), lambda p, i: (i, p + pairs)),
        ],
        out_specs=[
            own,
            pl.BlockSpec((block, 2 * HD), lambda p, i: (i, p)),
            pl.BlockSpec((block, 2 * HD), lambda p, i: (i, p)),
        ],
        out_shape=[
            jax.ShapeDtypeStruct((rows, width), jnp.bfloat16),
            jax.ShapeDtypeStruct((length, width), jnp.bfloat16),
            jax.ShapeDtypeStruct((length, width), jnp.bfloat16),
        ],
        scratch_shapes=[
            pltpu.VMEM((2 * HD, rows), jnp.float32),
            pltpu.VMEM((8, rows), jnp.float32),
        ],
        compiler_params=pltpu.CompilerParams(vmem_limit_bytes=VMEM_LIMIT),
        cost_estimate=pl.CostEstimate(
            flops=40 * rows * length * width,
            bytes_accessed=8 * length * width + 8 * rows * width,
            transcendentals=rows * length * width // HD,
        ),
        name="attend_back",
    )(query, grads, outs, lse, keys, keys)


def gelu_parts(values):
    cdf = 0.5 + 0.5 * lax.erf(values * (0.5**0.5))
    slope = cdf + values * ((2.0 * math.pi) ** -0.5) * jnp.exp(-0.5 * values * values)
    return (values * cdf, slope)


def half_turn(chunk):
    lanes = lax.broadcasted_iota(jnp.int32, chunk.shape, 1)
    half = HD // 2
    ahead = pltpu.roll(chunk, chunk.shape[1] - half, axis=1)
    behind = pltpu.roll(chunk, half, axis=1)
    return jnp.where(lanes % HD < half, ahead, behind)


def project_kernel(x_ref, gain_ref, w_ref, cos_ref, sin_ref, in_ref, q_ref, kv_ref):
    normed, _ = normalize(x_ref[...].astype(jnp.float32))
    attn_in = (normed * gain_ref[...]).astype(jnp.bfloat16)
    in_ref[...] = attn_in
    width = x_ref.shape[1]
    cosine, sine = cos_ref[...], sin_ref[...]
    for part, target, start in ((0, q_ref, 0), (1, kv_ref, 0), (2, kv_ref, width)):
        mixed = dot_nn(attn_in, w_ref[:, part * width : (part + 1) * width])
        for at in range(0, width, 2 * HD):
            chunk = mixed[:, at : at + 2 * HD]
            if part < 2:
                chunk = chunk * cosine + half_turn(chunk) * sine
            target[:, start + at : start + at + 2 * HD] = chunk.astype(jnp.bfloat16)


def project(inputs, gain, weights, cosine, sine, block):
    rows, width = inputs.shape
    by_rows = lambda columns: pl.BlockSpec((block, columns), lambda i: (i, 0))
    whole = lambda array: pl.BlockSpec(array.shape, lambda i: (0, 0))
    return pl.pallas_call(
        project_kernel,
        grid=(rows // block,),
        in_specs=[
            by_rows(width),
            whole(gain),
            whole(weights),
            by_rows(2 * HD),
            by_rows(2 * HD),
        ],
        out_specs=[by_rows(width), by_rows(width), by_rows(2 * width)],
        out_shape=[
            jax.ShapeDtypeStruct((rows, width), jnp.bfloat16),
            jax.ShapeDtypeStruct((rows, width), jnp.bfloat16),
            jax.ShapeDtypeStruct((rows, 2 * width), jnp.bfloat16),
        ],
        compiler_params=pltpu.CompilerParams(vmem_limit_bytes=VMEM_LIMIT),
        cost_estimate=pl.CostEstimate(
            flops=6 * rows * width * width, bytes_accessed=14 * rows * width, transcendentals=0
        ),
        name="project",
    )(inputs, gain, weights, cosine, sine)


def feed_kernel(
    x_ref, attn_ref, g_ref, gain_ref, wo_ref, wi_ref, wd_ref,
    out_ref, fin_ref, prod_ref, gmix_ref, ghid_ref, gbr_ref, gattn_ref, ggain_ref,
):
    @pl.when(pl.program_id(0) == 0)
    def _():
        ggain_ref[...] = jnp.zeros_like(ggain_ref)

    gain = gain_ref[...]
    hidden = x_ref[...].astype(jnp.float32) + dot_nn(attn_ref[...], wo_ref[...])
    normed, inverse = normalize(hidden)
    ffn_in = (normed * gain).astype(jnp.bfloat16)
    fin_ref[...] = ffn_in
    grads = g_ref[...]
    gate_part = dot_nn(ffn_in, wi_ref[:, :FF])
    up_part = dot_nn(ffn_in, wi_ref[:, FF:])
    activated, slope = gelu_parts(gate_part)
    product = (activated * up_part).astype(jnp.bfloat16)
    prod_ref[...] = product
    out_ref[...] = (hidden + dot_nt(product, wd_ref[...])).astype(jnp.bfloat16)
    grad_product = dot_nn(grads, wd_ref[...])
    grad_gate = (grad_product * up_part * slope).astype(jnp.bfloat16)
    grad_up = (grad_product * activated).astype(jnp.bfloat16)
    gmix_ref[:, :FF] = grad_gate
    gmix_ref[:, FF:] = grad_up
    grad_normed = dot_nt(grad_gate, wi_ref[:, :FF]) + dot_nt(grad_up, wi_ref[:, FF:])
    ggain_ref[0:1, :] += jnp.sum(grad_normed * normed, axis=0, keepdims=True)
    grad_hidden = grads.astype(jnp.float32) + norm_back(grad_normed, normed, inverse, gain)
    ghid_ref[...] = grad_hidden
    branch = grad_hidden.astype(jnp.bfloat16)
    gbr_ref[...] = branch
    gattn_ref[...] = dot_nt(branch, wo_ref[...]).astype(jnp.bfloat16)


def feed(inputs, attn_out, grads, gain, w_out, w_in, turned_down, block):
    rows, width = inputs.shape
    by_rows = lambda columns: pl.BlockSpec((block, columns), lambda i: (i, 0))
    whole = lambda array: pl.BlockSpec(array.shape, lambda i: (0, 0))
    like = lambda columns, kind=jnp.bfloat16: jax.ShapeDtypeStruct((rows, columns), kind)
    return pl.pallas_call(
        feed_kernel,
        grid=(rows // block,),
        in_specs=[by_rows(width)] * 3 + [whole(item) for item in (gain, w_out, w_in, turned_down)],
        out_specs=[
            by_rows(width),
            by_rows(width),
            by_rows(FF),
            by_rows(2 * FF),
            by_rows(width),
            by_rows(width),
            by_rows(width),
            pl.BlockSpec((8, width), lambda i: (0, 0)),
        ],
        out_shape=[
            like(width),
            like(width),
            like(FF),
            like(2 * FF),
            like(width, jnp.float32),
            like(width),
            like(width),
            jax.ShapeDtypeStruct((8, width), jnp.float32),
        ],
        compiler_params=pltpu.CompilerParams(vmem_limit_bytes=VMEM_LIMIT),
        cost_estimate=pl.CostEstimate(
            flops=4 * rows * width * (width + 3 * FF),
            bytes_accessed=30 * rows * width,
            transcendentals=2 * rows * FF,
        ),
        name="feed",
    )(inputs, attn_out, grads, gain, w_out, w_in, turned_down)


def finish_kernel(
    x_ref, ghid_ref, dq_ref, dk_ref, dv_ref, kv_ref, cos_ref, sin_ref, gain_ref, w_ref,
    raw_ref, gin_ref, ggain_ref,
):
    @pl.when(pl.program_id(0) == 0)
    def _():
        ggain_ref[...] = jnp.zeros_like(ggain_ref)

    width = x_ref.shape[1]
    cosine, sine = cos_ref[...], sin_ref[...]
    for part in range(3):
        for at in range(0, width, 2 * HD):
            if part == 0:
                chunk = dq_ref[:, at : at + 2 * HD].astype(jnp.float32)
            else:
                held = dk_ref if part == 1 else dv_ref
                start = (part - 1) * width + at
                chunk = held[:, at : at + 2 * HD].astype(jnp.float32)
                chunk = chunk + kv_ref[:, start : start + 2 * HD].astype(jnp.float32)
            if part < 2:
                chunk = chunk * cosine - half_turn(chunk) * sine
            start = part * width + at
            raw_ref[:, start : start + 2 * HD] = chunk.astype(jnp.bfloat16)
    grad_normed = dot_nt(raw_ref[...], w_ref[...])
    normed, inverse = normalize(x_ref[...].astype(jnp.float32))
    ggain_ref[0:1, :] += jnp.sum(grad_normed * normed, axis=0, keepdims=True)
    gin_ref[...] = ghid_ref[...] + norm_back(grad_normed, normed, inverse, gain_ref[...])


def finish(inputs, grad_hidden, grad_query, grad_keys, grad_values, received, cosine, sine, gain, weights, block):
    rows, width = inputs.shape
    by_rows = lambda columns: pl.BlockSpec((block, columns), lambda i: (i, 0))
    whole = lambda array: pl.BlockSpec(array.shape, lambda i: (0, 0))
    return pl.pallas_call(
        finish_kernel,
        grid=(rows // block,),
        in_specs=[by_rows(width)] * 5
        + [by_rows(2 * width), by_rows(2 * HD), by_rows(2 * HD), whole(gain), whole(weights)],
        out_specs=[
            by_rows(3 * width),
            by_rows(width),
            pl.BlockSpec((8, width), lambda i: (0, 0)),
        ],
        out_shape=[
            jax.ShapeDtypeStruct((rows, 3 * width), jnp.bfloat16),
            jax.ShapeDtypeStruct((rows, width), jnp.float32),
            jax.ShapeDtypeStruct((8, width), jnp.float32),
        ],
        compiler_params=pltpu.CompilerParams(vmem_limit_bytes=VMEM_LIMIT),
        cost_estimate=pl.CostEstimate(
            flops=6 * rows * width * width, bytes_accessed=26 * rows * width, transcendentals=0
        ),
        name="finish",
    )(inputs, grad_hidden, grad_query, grad_keys, grad_values, received, cosine, sine, gain, weights)


def swap_chips(values):
    return lax.ppermute(values, "seq", [(0, 2), (2, 0), (1, 3), (3, 1)])


def swap_cores(values):
    return lax.ppermute(values, "seq", [(0, 1), (1, 0), (2, 3), (3, 2)])


def take(values, which):
    return jnp.where(which == 0, values[0], values[1])


def gather(values):
    return lax.all_gather(values, "dp", axis=0, tiled=True)


def sum_shares(partial):
    core = lax.axis_index("seq") % 2
    half = partial.shape[1] // 2
    halves = (partial[:, :half].astype(jnp.bfloat16), partial[:, half:].astype(jnp.bfloat16))
    theirs = take(halves, 1 - core)
    mine = jnp.where(core == 0, partial[:, :half], partial[:, half:])
    mine = (mine + swap_cores(theirs).astype(jnp.float32)).astype(jnp.bfloat16)
    share = lax.psum_scatter(mine, "dp", scatter_dimension=0, tiled=True)
    share = share.astype(jnp.float32) + swap_chips(share).astype(jnp.float32)
    share = share.astype(jnp.bfloat16)
    other = swap_cores(share)
    both = jnp.where(
        core == 0,
        jnp.concatenate([share, other], axis=1),
        jnp.concatenate([other, share], axis=1),
    )
    return both.astype(jnp.float32)


def give_back(values, chip, tokens):
    mine, theirs = values[:tokens], swap_chips(values[tokens:])
    return jnp.where(chip == 0, jnp.stack([mine, theirs]), jnp.stack([theirs, mine]))


def shards(layer_input, cotangent, norm_gain1, w_qkv, w_out, norm_gain2, w_in, w_down):
    seq_count, tokens_dev, width = layer_input.shape
    index = lax.axis_index("seq")
    chip = index // 2
    rows = seq_count * tokens_dev
    sent_inputs = swap_chips(take(layer_input, 1 - chip))
    proj_qkv = gather(w_qkv)
    gains = gather(jnp.stack([norm_gain1, norm_gain2], axis=1)).astype(jnp.float32)
    gain_one, gain_two = gains[:, 0][None], gains[:, 1][None]
    proj_out = gather(w_out)
    proj_in = gather(w_in)
    turned_down = gather(w_down.T)
    inputs = jnp.concatenate([take(layer_input, chip), sent_inputs], axis=0)
    grad_output = jnp.concatenate(
        [take(cotangent, chip), swap_chips(take(cotangent, 1 - chip))], axis=0
    )
    local = jnp.arange(tokens_dev, dtype=jnp.int32)
    positions = jnp.concatenate([index * tokens_dev + local, (index ^ 2) * tokens_dev + local])
    cosine, sine = rope_tables(positions)
    half = HD // 2
    sine = jnp.concatenate([-sine[:, :half], sine[:, half:]], axis=1)
    cosine = jnp.concatenate([cosine, cosine], axis=1)
    sine = jnp.concatenate([sine, sine], axis=1)
    block = min(256, rows)
    attn_in, query, keys = project(inputs, gain_one, proj_qkv, cosine, sine, block)
    all_keys = jnp.concatenate([keys, swap_cores(keys)], axis=0)
    attn_out, lse = attend(query, all_keys, all_keys, block)
    output, ffn_in, product, grad_mixed_ffn, grad_hidden, grad_branch, grad_attn, gain_sum_two = feed(
        inputs, attn_out, grad_output, gain_two, proj_out, proj_in, turned_down, block
    )
    result = give_back(output, chip, tokens_dev)
    grad_down = contract_rows(grad_output, product)
    grad_in = contract_rows(ffn_in, grad_mixed_ffn)
    grad_proj_out = contract_rows(attn_out, grad_branch)
    early = sum_shares(jnp.concatenate([grad_in, grad_down, grad_proj_out], axis=1))
    total_in = early[:, : 2 * FF]
    total_down = early[:, 2 * FF : 3 * FF].T
    total_out = early[:, 3 * FF :]
    grad_query, grad_keys, grad_values = attend_back(
        query, grad_attn, attn_out, lse, all_keys, 512
    )
    received = swap_cores(jnp.concatenate([grad_keys[rows:], grad_values[rows:]], axis=1))
    grad_raw, grad_inputs, gain_sum_one = finish(
        inputs, grad_hidden, grad_query, grad_keys, grad_values, received,
        cosine, sine, gain_one, proj_qkv, block,
    )
    total_qkv = sum_shares(contract_rows(attn_in, grad_raw))
    grad_inputs = give_back_wide(grad_inputs, chip, tokens_dev)
    gain_totals = lax.psum(
        lax.psum_scatter(
            jnp.stack([gain_sum_one[0], gain_sum_two[0]], axis=1), "dp", scatter_dimension=0, tiled=True
        ),
        "seq",
    )
    return (
        result,
        grad_inputs,
        gain_totals[:, 0],
        total_qkv,
        total_out,
        gain_totals[:, 1],
        total_in,
        total_down,
    )


def give_back_wide(values, chip, tokens):
    mine = values[:tokens]
    theirs = swap_chips(values[tokens:].astype(jnp.bfloat16)).astype(jnp.float32)
    return jnp.where(chip == 0, jnp.stack([mine, theirs]), jnp.stack([theirs, mine]))


def solution(mesh):
    in_specs = (
        P("dp", "seq", None),
        P("dp", "seq", None),
        P("dp"),
        P("dp", None),
        P("dp", None),
        P("dp"),
        P("dp", None),
        P(None, "dp"),
    )
    out_specs = (
        P("dp", "seq", None),
        P("dp", "seq", None),
        P("dp"),
        P("dp", None),
        P("dp", None),
        P("dp"),
        P("dp", None),
        P(None, "dp"),
    )
    return jax.shard_map(shards, mesh=mesh, in_specs=in_specs, out_specs=out_specs, check_vma=False)
```

```python
import functools
import math

import jax
import jax.numpy as jnp
from jax import lax
from jax.experimental import pallas as pl
from jax.experimental.pallas import tpu as pltpu
from jax.sharding import PartitionSpec as P

H = 12
HD = 64
FF = 1152


rope_base = 160000.0
norm_eps = 1e-05


def normalize(values):
    centre = values - jnp.mean(values, axis=-1, keepdims=True)
    inverse = lax.rsqrt(jnp.mean(centre * centre, axis=-1, keepdims=True) + norm_eps)
    return (centre * inverse, inverse)


def norm_back(grad_normed, normed, inverse, gain):
    scaled = grad_normed * gain
    first = jnp.mean(scaled, axis=-1, keepdims=True)
    second = jnp.mean(scaled * normed, axis=-1, keepdims=True)
    return inverse * (scaled - first - normed * second)


def rope_tables(positions):
    half = HD // 2
    freqs = rope_base ** (-(jnp.arange(half, dtype=jnp.float32) * 2.0) / HD)
    angles = positions.astype(jnp.float32)[:, None] * freqs[None, :]
    angles = jnp.concatenate([angles, angles], axis=-1)
    return (jnp.cos(angles), jnp.sin(angles))


def rotate(values, cosine, sine):
    half = values.shape[-1] // 2
    turned = jnp.concatenate([-values[..., half:], values[..., :half]], axis=-1)
    return values * cosine[:, None, :] + turned * sine[:, None, :]


def rotate_back(grads, cosine, sine):
    half = grads.shape[-1] // 2
    moved = grads * sine[:, None, :]
    turned = jnp.concatenate([moved[..., half:], -moved[..., :half]], axis=-1)
    return grads * cosine[:, None, :] + turned


def exact_gelu(values):
    return jax.nn.gelu(values, approximate=False)


def contract_rows(left, right):
    return lax.dot_general(
        left, right, (((0,), (0,)), ((), ())), preferred_element_type=jnp.float32
    )


def times_transpose(left, right):
    return lax.dot_general(
        left, right, (((1,), (1,)), ((), ())), preferred_element_type=jnp.float32
    )


SCALE = HD ** (-0.5)
TO_BASE2 = SCALE * math.log2(math.e)
VMEM_LIMIT = 56 * 1024 * 1024


def dot_nt(left, right):
    return lax.dot_general(
        left, right, (((1,), (1,)), ((), ())), preferred_element_type=jnp.float32
    )


def dot_nn(left, right):
    return lax.dot_general(
        left, right, (((1,), (0,)), ((), ())), preferred_element_type=jnp.float32
    )


def only_head(values, head):
    lanes = lax.broadcasted_iota(jnp.int32, values.shape, 1)
    mine = (lanes < HD) if head == 0 else (lanes >= HD)
    return jnp.where(mine, values, jnp.zeros_like(values))


def join_heads(first, second):
    lanes = lax.broadcasted_iota(jnp.int32, first.shape, 1)
    return jnp.where(lanes < HD, first, second)


def attend_kernel(q_ref, k_ref, v_ref, out_ref, lse_ref, wide_ref):
    @pl.when(pl.program_id(1) == 0)
    def _():
        wide_ref[:, : 2 * HD] = v_ref[...]
        wide_ref[:, 2 * HD :] = jnp.ones_like(v_ref)

    outs, sums = [], []
    for head in range(2):
        scores = dot_nt(only_head(q_ref[...], head), k_ref[...])
        top = jnp.max(scores, axis=-1, keepdims=True)
        weights = jnp.exp2((scores - top) * TO_BASE2).astype(jnp.bfloat16)
        both = dot_nn(weights, wide_ref[...])
        total = both[:, 2 * HD :]
        outs.append(both[:, : 2 * HD] / total)
        sums.append(top * TO_BASE2 + jnp.log2(total))
    out_ref[...] = join_heads(outs[0], outs[1]).astype(jnp.bfloat16)
    turned = join_heads(sums[0], sums[1]).T
    lse_ref[0, 0:1, :] = turned[0:1]
    lse_ref[0, 1:2, :] = turned[HD : HD + 1]


def attend(query, keys, block, first):
    rows = query.shape[0]
    length = keys.shape[0]
    width = keys.shape[1] // 2
    pairs = width // (2 * HD)
    return pl.pallas_call(
        attend_kernel,
        grid=(pairs, rows // block),
        in_specs=[
            pl.BlockSpec((block, 2 * HD), lambda p, i: (i, p + first)),
            pl.BlockSpec((length, 2 * HD), lambda p, i: (0, p)),
            pl.BlockSpec((length, 2 * HD), lambda p, i: (0, p + pairs)),
        ],
        out_specs=[
            pl.BlockSpec((block, 2 * HD), lambda p, i: (i, p)),
            pl.BlockSpec((1, 8, block), lambda p, i: (p, 0, i)),
        ],
        out_shape=[
            jax.ShapeDtypeStruct((rows, width), jnp.bfloat16),
            jax.ShapeDtypeStruct((pairs, 8, rows), jnp.float32),
        ],
        scratch_shapes=[pltpu.VMEM((length, 4 * HD), jnp.bfloat16)],
        compiler_params=pltpu.CompilerParams(vmem_limit_bytes=VMEM_LIMIT),
        cost_estimate=pl.CostEstimate(
            flops=16 * rows * length * width,
            bytes_accessed=4 * length * width + 4 * rows * width,
            transcendentals=rows * length * width // HD,
        ),
        name="attend",
    )(query, keys, keys)


def attend_back_kernel(
    q_ref, do_ref, o_ref, lse_ref, k_ref, v_ref, dq_ref, dk_ref, dv_ref, acc_ref, delta_ref
):
    step = pl.program_id(1)

    @pl.when(step == 0)
    def _():
        both = (do_ref[...].astype(jnp.float32) * o_ref[...].astype(jnp.float32)).T
        delta_ref[0:1, :] = jnp.sum(both[:HD], axis=0, keepdims=True)
        delta_ref[1:2, :] = jnp.sum(both[HD:], axis=0, keepdims=True)
        acc_ref[...] = jnp.zeros_like(acc_ref)

    keys = k_ref[...]
    turned_keys = keys.astype(jnp.float32).T.astype(jnp.bfloat16)
    grad_keys, grad_values = [], []
    for head in range(2):
        scores = dot_nt(keys, only_head(q_ref[...], head))
        probs = jnp.exp2(scores * TO_BASE2 - lse_ref[0, head : head + 1, :])
        grad_probs = dot_nt(v_ref[...], only_head(do_ref[...], head))
        grad_scores = (probs * (grad_probs - delta_ref[head : head + 1, :])).astype(jnp.bfloat16)
        grad_values.append(dot_nn(probs.astype(jnp.bfloat16), do_ref[...]))
        grad_keys.append(dot_nn(grad_scores, q_ref[...]))
        acc_ref[head * HD : (head + 1) * HD, :] += dot_nn(
            turned_keys[head * HD : (head + 1) * HD], grad_scores
        )
    dv_ref[...] = join_heads(grad_values[0], grad_values[1]).astype(jnp.bfloat16)
    dk_ref[...] = (join_heads(grad_keys[0], grad_keys[1]) * SCALE).astype(jnp.bfloat16)

    @pl.when(step == pl.num_programs(1) - 1)
    def _():
        dq_ref[...] = (acc_ref[...].T * SCALE).astype(jnp.bfloat16)


def attend_back(query, grads, outs, lse, keys, block, first):
    rows = query.shape[0]
    length = keys.shape[0]
    width = keys.shape[1] // 2
    pairs = width // (2 * HD)
    own = pl.BlockSpec((rows, 2 * HD), lambda p, i: (0, p + first))
    return pl.pallas_call(
        attend_back_kernel,
        grid=(pairs, length // block),
        in_specs=[
            own,
            own,
            pl.BlockSpec((rows, 2 * HD), lambda p, i: (0, p)),
            pl.BlockSpec((1, 8, rows), lambda p, i: (p, 0, 0)),
            pl.BlockSpec((block, 2 * HD), lambda p, i: (i, p)),
            pl.BlockSpec((block, 2 * HD), lambda p, i: (i, p + pairs)),
        ],
        out_specs=[
            pl.BlockSpec((rows, 2 * HD), lambda p, i: (0, p)),
            pl.BlockSpec((block, 2 * HD), lambda p, i: (i, p)),
            pl.BlockSpec((block, 2 * HD), lambda p, i: (i, p)),
        ],
        out_shape=[
            jax.ShapeDtypeStruct((rows, width), jnp.bfloat16),
            jax.ShapeDtypeStruct((length, width), jnp.bfloat16),
            jax.ShapeDtypeStruct((length, width), jnp.bfloat16),
        ],
        scratch_shapes=[
            pltpu.VMEM((2 * HD, rows), jnp.float32),
            pltpu.VMEM((8, rows), jnp.float32),
        ],
        compiler_params=pltpu.CompilerParams(vmem_limit_bytes=VMEM_LIMIT),
        cost_estimate=pl.CostEstimate(
            flops=40 * rows * length * width,
            bytes_accessed=8 * length * width + 8 * rows * width,
            transcendentals=rows * length * width // HD,
        ),
        name="attend_back",
    )(query, grads, outs, lse, keys, keys)


def gelu_parts(values):
    cdf = 0.5 + 0.5 * lax.erf(values * (0.5**0.5))
    slope = cdf + values * ((2.0 * math.pi) ** -0.5) * jnp.exp(-0.5 * values * values)
    return (values * cdf, slope)


def half_turn(chunk):
    lanes = lax.broadcasted_iota(jnp.int32, chunk.shape, 1)
    half = HD // 2
    ahead = pltpu.roll(chunk, chunk.shape[1] - half, axis=1)
    behind = pltpu.roll(chunk, half, axis=1)
    return jnp.where(lanes % HD < half, ahead, behind)


def project_kernel(x_ref, gain_ref, w_ref, cos_ref, sin_ref, in_ref, q_ref, one_ref, two_ref):
    normed, _ = normalize(x_ref[...].astype(jnp.float32))
    attn_in = (normed * gain_ref[...]).astype(jnp.bfloat16)
    in_ref[...] = attn_in
    width = x_ref.shape[1]
    cosine, sine = cos_ref[...], sin_ref[...]
    share = width // 2
    for part in range(3):
        mixed = dot_nn(attn_in, w_ref[:, part * width : (part + 1) * width])
        for at in range(0, width, 2 * HD):
            chunk = mixed[:, at : at + 2 * HD]
            if part < 2:
                chunk = chunk * cosine + half_turn(chunk) * sine
            target, start = (q_ref, at)
            if part > 0:
                target = (one_ref, two_ref)[at // share]
                start = (part - 1) * share + at % share
            target[:, start : start + 2 * HD] = chunk.astype(jnp.bfloat16)


def project(inputs, gain, weights, cosine, sine, block):
    rows, width = inputs.shape
    by_rows = lambda columns: pl.BlockSpec((block, columns), lambda i: (i, 0))
    whole = lambda array: pl.BlockSpec(array.shape, lambda i: (0, 0))
    return pl.pallas_call(
        project_kernel,
        grid=(rows // block,),
        in_specs=[
            by_rows(width),
            whole(gain),
            whole(weights),
            by_rows(2 * HD),
            by_rows(2 * HD),
        ],
        out_specs=[by_rows(width)] * 4,
        out_shape=[jax.ShapeDtypeStruct((rows, width), jnp.bfloat16)] * 4,
        compiler_params=pltpu.CompilerParams(vmem_limit_bytes=VMEM_LIMIT),
        cost_estimate=pl.CostEstimate(
            flops=6 * rows * width * width, bytes_accessed=14 * rows * width, transcendentals=0
        ),
        name="project",
    )(inputs, gain, weights, cosine, sine)


def feed_kernel(
    x_ref, one_ref, two_ref, g_ref, gain_ref, wo_ref, wi_ref, wd_ref,
    out_ref, fin_ref, prod_ref, gmix_ref, ghid_ref, gbr_ref, gattn_ref, ggain_ref,
):
    @pl.when(pl.program_id(0) == 0)
    def _():
        ggain_ref[...] = jnp.zeros_like(ggain_ref)

    gain = gain_ref[...]
    attn = jnp.concatenate([one_ref[...], two_ref[...]], axis=1)
    hidden = x_ref[...].astype(jnp.float32) + dot_nn(attn, wo_ref[...])
    normed, inverse = normalize(hidden)
    ffn_in = (normed * gain).astype(jnp.bfloat16)
    fin_ref[...] = ffn_in
    grads = g_ref[...]
    gate_part = dot_nn(ffn_in, wi_ref[:, :FF])
    up_part = dot_nn(ffn_in, wi_ref[:, FF:])
    activated, slope = gelu_parts(gate_part)
    product = (activated * up_part).astype(jnp.bfloat16)
    prod_ref[...] = product
    out_ref[...] = (hidden + dot_nt(product, wd_ref[...])).astype(jnp.bfloat16)
    grad_product = dot_nn(grads, wd_ref[...])
    grad_gate = (grad_product * up_part * slope).astype(jnp.bfloat16)
    grad_up = (grad_product * activated).astype(jnp.bfloat16)
    gmix_ref[:, :FF] = grad_gate
    gmix_ref[:, FF:] = grad_up
    grad_normed = dot_nt(grad_gate, wi_ref[:, :FF]) + dot_nt(grad_up, wi_ref[:, FF:])
    ggain_ref[0:1, :] += jnp.sum(grad_normed * normed, axis=0, keepdims=True)
    grad_hidden = grads.astype(jnp.float32) + norm_back(grad_normed, normed, inverse, gain)
    ghid_ref[...] = grad_hidden
    branch = grad_hidden.astype(jnp.bfloat16)
    gbr_ref[...] = branch
    gattn_ref[...] = dot_nt(branch, wo_ref[...]).astype(jnp.bfloat16)


def feed(inputs, attn_one, attn_two, grads, gain, w_out, w_in, turned_down, block):
    rows, width = inputs.shape
    by_rows = lambda columns: pl.BlockSpec((block, columns), lambda i: (i, 0))
    whole = lambda array: pl.BlockSpec(array.shape, lambda i: (0, 0))
    like = lambda columns, kind=jnp.bfloat16: jax.ShapeDtypeStruct((rows, columns), kind)
    return pl.pallas_call(
        feed_kernel,
        grid=(rows // block,),
        in_specs=[by_rows(width), by_rows(width // 2), by_rows(width // 2), by_rows(width)]
        + [whole(item) for item in (gain, w_out, w_in)]
        + [pl.BlockSpec((width, FF), lambda i: (0, 0))],
        out_specs=[
            by_rows(width),
            by_rows(width),
            by_rows(FF),
            by_rows(2 * FF),
            by_rows(width),
            by_rows(width),
            by_rows(width),
            pl.BlockSpec((8, width), lambda i: (0, 0)),
        ],
        out_shape=[
            like(width),
            like(width),
            like(FF),
            like(2 * FF),
            like(width, jnp.float32),
            like(width),
            like(width),
            jax.ShapeDtypeStruct((8, width), jnp.float32),
        ],
        compiler_params=pltpu.CompilerParams(vmem_limit_bytes=VMEM_LIMIT),
        cost_estimate=pl.CostEstimate(
            flops=4 * rows * width * (width + 3 * FF),
            bytes_accessed=30 * rows * width,
            transcendentals=2 * rows * FF,
        ),
        name="feed",
    )(inputs, attn_one, attn_two, grads, gain, w_out, w_in, turned_down)


def finish_kernel(*refs):
    x_ref, ghid_ref = refs[:2]
    parts = (refs[2:6], refs[6:10])
    cos_ref, sin_ref, gain_ref, w_ref, raw_ref, gin_ref, ggain_ref = refs[10:]

    @pl.when(pl.program_id(0) == 0)
    def _():
        ggain_ref[...] = jnp.zeros_like(ggain_ref)

    width = x_ref.shape[1]
    share = width // 2
    cosine, sine = cos_ref[...], sin_ref[...]
    for part in range(3):
        for at in range(0, width, 2 * HD):
            dq_ref, dk_ref, dv_ref, kv_ref = parts[at // share]
            here = at % share
            held = (dq_ref, dk_ref, dv_ref)[part]
            chunk = held[:, here : here + 2 * HD].astype(jnp.float32)
            if part > 0:
                start = (part - 1) * share + here
                chunk = chunk + kv_ref[:, start : start + 2 * HD].astype(jnp.float32)
            if part < 2:
                chunk = chunk * cosine - half_turn(chunk) * sine
            start = part * width + at
            raw_ref[:, start : start + 2 * HD] = chunk.astype(jnp.bfloat16)
    grad_normed = dot_nt(raw_ref[...], w_ref[...])
    normed, inverse = normalize(x_ref[...].astype(jnp.float32))
    ggain_ref[0:1, :] += jnp.sum(grad_normed * normed, axis=0, keepdims=True)
    gin_ref[...] = ghid_ref[...] + norm_back(grad_normed, normed, inverse, gain_ref[...])


def finish(inputs, grad_hidden, parts, cosine, sine, gain, weights, block):
    rows, width = inputs.shape
    by_rows = lambda columns: pl.BlockSpec((block, columns), lambda i: (i, 0))
    whole = lambda array: pl.BlockSpec(array.shape, lambda i: (0, 0))
    return pl.pallas_call(
        finish_kernel,
        grid=(rows // block,),
        in_specs=[by_rows(width)] * 2
        + ([by_rows(width // 2)] * 3 + [by_rows(width)]) * 2
        + [by_rows(2 * HD), by_rows(2 * HD), whole(gain), whole(weights)],
        out_specs=[
            by_rows(3 * width),
            by_rows(width),
            pl.BlockSpec((8, width), lambda i: (0, 0)),
        ],
        out_shape=[
            jax.ShapeDtypeStruct((rows, 3 * width), jnp.bfloat16),
            jax.ShapeDtypeStruct((rows, width), jnp.float32),
            jax.ShapeDtypeStruct((8, width), jnp.float32),
        ],
        compiler_params=pltpu.CompilerParams(vmem_limit_bytes=VMEM_LIMIT),
        cost_estimate=pl.CostEstimate(
            flops=6 * rows * width * width, bytes_accessed=26 * rows * width, transcendentals=0
        ),
        name="finish",
    )(inputs, grad_hidden, *parts[0], *parts[1], cosine, sine, gain, weights)


def swap_chips(values):
    return lax.ppermute(values, "seq", [(0, 2), (2, 0), (1, 3), (3, 1)])


def swap_cores(values):
    return lax.ppermute(values, "seq", [(0, 1), (1, 0), (2, 3), (3, 2)])


def take(values, which):
    return jnp.where(which == 0, values[0], values[1])


def by_core(values):
    core = lax.axis_index("seq") % 2
    half = values.shape[1] // 2
    first, second = values[:, :half], values[:, half:]
    return jnp.where(core == 0, first, second), jnp.where(core == 0, second, first)


def join_cores(mine, theirs):
    core = lax.axis_index("seq") % 2
    first = jnp.where(core == 0, mine, theirs)
    second = jnp.where(core == 0, theirs, mine)
    return jnp.concatenate([first, second], axis=1)


def send_rows(values):
    parts = lax.axis_size("dp")
    pieces = values.reshape(parts, values.shape[0] // parts, values.shape[1])
    return lax.all_to_all(pieces, "dp", split_axis=0, concat_axis=0, tiled=True)


def finish_halves(pieces):
    share = jnp.sum(pieces.astype(jnp.float32), axis=0)
    share = share + swap_chips(share.astype(jnp.bfloat16)).astype(jnp.float32)
    share = share.astype(jnp.bfloat16)
    return share, swap_cores(share)


def finish_sum(pieces):
    return join_cores(*finish_halves(pieces)).astype(jnp.float32)


def give_back(values, chip, tokens):
    mine, theirs = values[:tokens], swap_chips(values[tokens:])
    return jnp.where(chip == 0, jnp.stack([mine, theirs]), jnp.stack([theirs, mine]))


def shards(layer_input, cotangent, norm_gain1, w_qkv, w_out, norm_gain2, w_in, w_down):
    seq_count, tokens_dev, width = layer_input.shape
    index = lax.axis_index("seq")
    chip = index // 2
    rows = seq_count * tokens_dev
    sent_inputs = swap_chips(take(layer_input, 1 - chip))
    columns = w_qkv.shape[1] // 2
    column = lambda values: jnp.pad(values[:, None], ((0, 0), (0, 2 * HD - 1)))
    own_qkv, _ = by_core(
        jnp.concatenate(
            [w_qkv[:, :columns], column(norm_gain1), w_qkv[:, columns:], column(norm_gain2)], axis=1
        )
    )
    half_qkv = lax.all_gather(own_qkv, "dp", axis=0, tiled=True)
    other_qkv = swap_cores(half_qkv)
    proj_qkv = join_cores(half_qkv[:, :columns], other_qkv[:, :columns])
    gains = join_cores(half_qkv[:, columns : columns + 1], other_qkv[:, columns : columns + 1])
    gains = gains.astype(jnp.float32)
    gain_one, gain_two = gains[:, 0][None], gains[:, 1][None]
    down = -(-FF // (4 * HD)) * 4 * HD
    padded = lambda values: jnp.pad(values, ((0, 0), (0, down - FF)))
    halves = [by_core(item)[0] for item in (w_in, w_out, padded(w_down.T))]
    half_rest = lax.all_gather(jnp.concatenate(halves, axis=1), "dp", axis=0, tiled=True)
    inputs = jnp.concatenate([take(layer_input, chip), sent_inputs], axis=0)
    grad_output = jnp.concatenate(
        [take(cotangent, chip), swap_chips(take(cotangent, 1 - chip))], axis=0
    )
    local = jnp.arange(tokens_dev, dtype=jnp.int32)
    positions = jnp.concatenate([index * tokens_dev + local, (index ^ 2) * tokens_dev + local])
    cosine, sine = rope_tables(positions)
    half = HD // 2
    sine = jnp.concatenate([-sine[:, :half], sine[:, half:]], axis=1)
    cosine = jnp.concatenate([cosine, cosine], axis=1)
    sine = jnp.concatenate([sine, sine], axis=1)
    block = min(256, rows)
    split = width // (4 * HD)
    attn_in, query, *keys = project(inputs, gain_one, proj_qkv, cosine, sine, block)
    keys = [jnp.concatenate([item, swap_cores(item)], axis=0) for item in keys]
    attn_one, lse_one = attend(query, keys[0], block, 0)
    half_rest, attn_one = lax.optimization_barrier((half_rest, attn_one))
    other_rest = swap_cores(half_rest)
    attn_two, lse_two = attend(query, keys[1], block, split)
    proj_in = join_cores(half_rest[:, :FF], other_rest[:, :FF])
    cut = FF + width // 2
    proj_out = join_cores(half_rest[:, FF:cut], other_rest[:, FF:cut])
    turned_down = join_cores(half_rest[:, cut:], other_rest[:, cut:])
    output, ffn_in, product, grad_mixed_ffn, grad_hidden, grad_branch, grad_attn, gain_sum_two = feed(
        inputs, attn_one, attn_two, grad_output, gain_two, proj_out, proj_in, turned_down, block
    )
    result = give_back(output, chip, tokens_dev)

    def ready(mine, theirs):
        return (mine + theirs.astype(jnp.float32)).astype(jnp.bfloat16)

    in_mine, in_theirs = by_core(contract_rows(ffn_in, grad_mixed_ffn))
    in_theirs = in_theirs.astype(jnp.bfloat16)
    in_theirs, product, grad_branch = lax.optimization_barrier((in_theirs, product, grad_branch))
    in_got = swap_cores(in_theirs)
    grad_down = padded(contract_rows(grad_output, product))
    grad_proj_out = jnp.concatenate(
        [contract_rows(attn_one, grad_branch), contract_rows(attn_two, grad_branch)], axis=0
    )
    down_mine, down_theirs = by_core(grad_down)
    out_mine, out_theirs = by_core(grad_proj_out)
    rest_theirs = jnp.concatenate([down_theirs, out_theirs], axis=1).astype(jnp.bfloat16)
    in_sum = ready(in_mine, in_got)
    in_sum, rest_theirs, grad_attn = lax.optimization_barrier((in_sum, rest_theirs, grad_attn))
    in_pieces = send_rows(in_sum)
    rest_got = swap_cores(rest_theirs)
    kv_block = min(512, 2 * rows)

    def back_part(grads, attn_out, lse, held, first):
        grad_query, grad_keys, grad_values = attend_back(
            query, grads, attn_out, lse, held, kv_block, first
        )
        received = swap_cores(jnp.concatenate([grad_keys[rows:], grad_values[rows:]], axis=1))
        return (grad_query, grad_keys, grad_values, received)

    part_one = back_part(grad_attn, attn_one, lse_one, keys[0], 0)
    rest_sum = ready(jnp.concatenate([down_mine, out_mine], axis=1), rest_got)
    rest_sum, in_pieces, grad_attn, result, _ = lax.optimization_barrier(
        (rest_sum, in_pieces, grad_attn, result, part_one[0])
    )
    rest_pieces = send_rows(rest_sum)
    part_two = back_part(grad_attn, attn_two, lse_two, keys[1], split)
    rest_pieces, last_query = lax.optimization_barrier((rest_pieces, part_two[0]))
    part_two = (last_query, *part_two[1:])
    grad_raw, grad_inputs, gain_sum_one = finish(
        inputs, grad_hidden, (part_one, part_two), cosine, sine, gain_one, proj_qkv, block
    )
    grad_proj_qkv = contract_rows(attn_in, grad_raw)
    late_mine, late_theirs = by_core(
        jnp.concatenate(
            [
                grad_proj_qkv[:, :columns],
                column(gain_sum_one[0]),
                grad_proj_qkv[:, columns:],
                column(gain_sum_two[0]),
            ],
            axis=1,
        )
    )
    late_got = swap_cores(late_theirs.astype(jnp.bfloat16))
    late_sum = ready(late_mine, late_got)
    grad_inputs = give_back_wide(grad_inputs, chip, tokens_dev)
    late_sum, grad_inputs = lax.optimization_barrier((late_sum, grad_inputs))
    late_pieces = send_rows(late_sum)
    total_in = finish_sum(in_pieces)
    rest_mine, rest_other = finish_halves(rest_pieces)
    half_down = down // 2
    total_down = join_cores(rest_mine[:, :half_down], rest_other[:, :half_down])[:, :FF]
    total_down = total_down.T.astype(jnp.float32)
    total_out = join_cores(rest_mine[:, half_down:], rest_other[:, half_down:]).astype(jnp.float32)
    late = finish_sum(late_pieces)
    total_qkv = jnp.concatenate(
        [late[:, :columns], late[:, columns + 2 * HD : 2 * columns + 2 * HD]], axis=1
    )
    total_one, total_two = late[:, columns], late[:, 2 * columns + 2 * HD]
    return (
        result,
        grad_inputs,
        total_one,
        total_qkv,
        total_out,
        total_two,
        total_in,
        total_down,
    )


def give_back_wide(values, chip, tokens):
    mine = values[:tokens]
    theirs = swap_chips(values[tokens:].astype(jnp.bfloat16)).astype(jnp.float32)
    return jnp.where(chip == 0, jnp.stack([mine, theirs]), jnp.stack([theirs, mine]))


def solution(mesh):
    in_specs = (
        P("dp", "seq", None),
        P("dp", "seq", None),
        P("dp"),
        P("dp", None),
        P("dp", None),
        P("dp"),
        P("dp", None),
        P(None, "dp"),
    )
    out_specs = (
        P("dp", "seq", None),
        P("dp", "seq", None),
        P("dp"),
        P("dp", None),
        P("dp", None),
        P("dp"),
        P("dp", None),
        P(None, "dp"),
    )
    return jax.shard_map(shards, mesh=mesh, in_specs=in_specs, out_specs=out_specs, check_vma=False)
```
